512 devices in a mesh: frame: 32 (over y, x, core), seq: 16 (over z).
Axes of the slice: x: 4, y: 4, z: 16, core: 2. Of those that a mesh axis runs over, the one named last changes fastest.
Arguments:
- queries: bfloat16 [32, 2048, 2048], P('frame', 'seq'), may hold values from -23 to 23
- key_proj: bfloat16 [32, 2048, 2048], P('frame', 'seq'), may hold values from -7 to 7
- values: bfloat16 [32, 2048, 2048], P('frame', 'seq'), may hold values from -6 to 6
- back_count: int32 [32], P('frame'), may hold values from 0 to 1
- ahead_count: int32 [32], P('frame'), may hold values from 0 to 1
- timestep: int32 [32], P('frame'), may hold values from 1 to 50
- latent: float32 [32, 2048, 64], P('frame', 'seq'), may hold values from -6 to 6
- noise_frame: float32 [2048, 64], P('seq'), may hold values from -6 to 6
- w_final: bfloat16 [2048, 64], replicated, may hold values from -0.5 to 0.5
Outputs:
- velocity: float32 [32, 2048, 64], P('frame', 'seq')
- new_queue: float32 [32, 2048, 64], P('frame', 'seq')
The draws below stay inside these ranges and needn't reach their ends.
All inputs are finite; a program needn't handle non-finite values.
Results may differ from the reference program's by a relative error of at most 0.0041.
Values may be sent and summed in bfloat16 or wider, within the bound.
A program may use at most 64 MiB of HBM per device.

```python
import jax
import jax.numpy as jnp
from jax import lax

H = 16
HD = 128
LAT = 64
STEPS = 50
TOK = 2048
FRAMES = 32


def paired_fields(key):
    shape = (FRAMES, TOK, H * HD)
    key_query = jax.random.fold_in(key, 11)
    key_keys = jax.random.fold_in(key, 12)
    made_queries = 1.6 * jax.random.truncated_normal(key_query, -4.0, 4.0, shape, jnp.float32)
    made_keys = 1.6 * jax.random.truncated_normal(key_keys, -4.0, 4.0, shape, jnp.float32)
    return (made_queries, made_keys)


def draw_queries(key, part):
    made_queries, made_keys = paired_fields(key)
    return made_queries.astype(jnp.bfloat16)


def draw_key_proj(key, part):
    made_queries, made_keys = paired_fields(key)
    return made_keys.astype(jnp.bfloat16)


def plant(result, key, least, high):
    dims = result.shape
    index_at = [jax.random.randint(jax.random.fold_in(key, axis), (), 0, dims[axis]) for axis in range(len(dims))]
    result = result.at[tuple(index_at)].set(least)
    longest = dims.index(max(dims))
    index_at[longest] = (index_at[longest] + 1) % dims[longest]
    return result.at[tuple(index_at)].set(high)


def block_levels(stream_key, extent, shards, low, largest):
    def one(position, parts):
        steps = jax.random.uniform(jax.random.fold_in(jax.random.fold_in(stream_key, 6), position), (parts,), jnp.float32, low / len(shards), largest / len(shards))
        return jnp.repeat(jnp.exp(steps), extent[position] // parts).reshape((-1,) + (1,) * (len(extent) - position - 1))

    loudness = one(*shards[0])
    for cut in shards[1:]:
        loudness = loudness * one(*cut)
    return loudness


def gaussian(own_key, dims, scale, bound, shards=(), kind=jnp.bfloat16):
    values = scale * jax.random.normal(own_key, dims, jnp.float32)
    if shards:
        values = values * block_levels(own_key, dims, shards, -0.22, 0.18)
    return jnp.clip(values, -bound, bound).astype(kind)


def setup_inputs(seed: int = 0) -> dict:
    keys = jax.random.split(jax.random.key(seed), 10)
    queries = draw_queries(jax.random.fold_in(keys[9], 71), 0)
    key_proj = draw_key_proj(jax.random.fold_in(keys[9], 71), 0)
    values = gaussian(keys[2], (FRAMES, TOK, H * HD), 1.0, 6.0, ((0, 32), (1, 16)))
    back_count = plant(jax.random.randint(keys[3], (FRAMES,), 0, 2), jax.random.fold_in(keys[3], 1), 0, 1).astype(jnp.int32)
    ahead_count = plant(jax.random.randint(keys[4], (FRAMES,), 0, 2), jax.random.fold_in(keys[4], 1), 0, 1).astype(jnp.int32)
    timestep = plant(jax.random.randint(keys[5], (FRAMES,), 1, STEPS + 1), jax.random.fold_in(keys[5], 1), 1, STEPS).astype(jnp.int32)
    latent = gaussian(keys[6], (FRAMES, TOK, LAT), 1.0, 6.0, ((0, 32), (1, 16)), jnp.float32)
    noise_frame = gaussian(keys[7], (TOK, LAT), 1.0, 6.0, ((0, 16),), jnp.float32)
    w_final = gaussian(keys[8], (H * HD, LAT), HD ** -0.5, 0.5)
    return {"queries": queries, "key_proj": key_proj, "values": values, "back_count": back_count, "ahead_count": ahead_count, "timestep": timestep, "latent": latent, "noise_frame": noise_frame, "w_final": w_final}


flow_shift = 7.0


def sigma_of(index):
    share = index.astype(jnp.float32) / STEPS
    return flow_shift * share / (1.0 + (flow_shift - 1.0) * share)


def reference(queries, key_proj, values, back_count, ahead_count, timestep, latent, noise_frame, w_final):
    frames = queries.shape[0]
    tok = queries.shape[1]
    zero_frame = jnp.zeros((1, tok, H * HD), jnp.bfloat16)
    keys_pad = jnp.concatenate([zero_frame, key_proj, zero_frame], axis=0)
    vals_pad = jnp.concatenate([zero_frame, values, zero_frame], axis=0)
    scale = HD ** -0.5

    def one_frame(place):
        key_win = lax.dynamic_slice_in_dim(keys_pad, place, 3, 0).reshape(3 * tok, H * HD)
        val_win = lax.dynamic_slice_in_dim(vals_pad, place, 3, 0).reshape(3 * tok, H * HD)
        query_frame = lax.dynamic_index_in_dim(queries, place, 0, keepdims=False)
        has_prev = jnp.logical_and(back_count[place] >= 1, place >= 1)
        has_next = jnp.logical_and(ahead_count[place] >= 1, place <= frames - 2)
        allowed = jnp.repeat(jnp.stack([has_prev, jnp.array(True), has_next]), tok)

        def one_head(head):
            start = (head * HD).astype(jnp.int32)
            query_head = lax.dynamic_slice_in_dim(query_frame, start, HD, 1)
            key_head = lax.dynamic_slice_in_dim(key_win, start, HD, 1)
            val_head = lax.dynamic_slice_in_dim(val_win, start, HD, 1)
            scores = jnp.dot(query_head, key_head.T, preferred_element_type=jnp.float32) * scale
            scores = jnp.where(allowed[None, :], scores, -jnp.inf)
            top = jnp.max(scores, axis=1, keepdims=True)
            expo = jnp.exp(scores - top)
            weights = (expo / jnp.sum(expo, axis=1, keepdims=True)).astype(jnp.bfloat16)
            return jnp.dot(weights, val_head, preferred_element_type=jnp.float32).astype(jnp.bfloat16)

        heads = lax.map(one_head, jnp.arange(H, dtype=jnp.int32))
        return jnp.transpose(heads, (1, 0, 2)).reshape(tok, H * HD)

    attended = lax.map(one_frame, jnp.arange(frames, dtype=jnp.int32))
    velocity = jnp.dot(attended.reshape(frames * tok, H * HD), w_final, preferred_element_type=jnp.float32).reshape(frames, tok, LAT)
    step_size = sigma_of(timestep - 1) - sigma_of(timestep)
    moved = latent + step_size[:, None, None] * velocity
    new_queue = jnp.concatenate([moved[1:], noise_frame[None]], axis=0)
    return velocity, new_queue
```

```python
import functools
import math

import jax
import jax.numpy as jnp
from jax import lax
from jax.experimental import pallas as pl
from jax.experimental.pallas import tpu as pltpu
from jax.sharding import PartitionSpec as P

HD = 128
TOKS = 128
LAT = 64
STEPS = 50
SHIFT = 7.0
RATE = HD ** (-0.5) * math.log2(math.e)
F32, BF16 = jnp.float32, jnp.bfloat16
CHUNK = 256
PAIR = 2 * TOKS
SUMS = 16
GROUPS = 4


def sigma_of(index):
    share = index / STEPS
    return SHIFT * share / (1.0 + (SHIFT - 1.0) * share)


def kernel(
    ns, nf, back_ref, ahead_ref, time_ref, q_hbm, k_hbm, v_ref, w_ref, latent_ref, noise_ref,
    vel_ref, new_ref,
    keys, vals, vsend, weighted, qbuf, osend, obuf, mine, theirs, s0, s1,
    own_sem, k_out, v_out, q_out, o_out, f_out, m_sems, k_in, v_in, q_in, o_in, f_in,
):
    place, here = lax.axis_index("frame"), lax.axis_index("seq")
    after, before = lax.rem(place + 1, nf), lax.rem(place + nf - 1, nf)
    half = ns // 2
    per = ns // GROUPS
    toks = ns * TOKS

    def offset(j):
        return jnp.where(j == 0, 0, jnp.where(j % 2 == 0, half - j // 2, (j - 1) // 2 - half))

    def peer(j, sign):
        return lax.rem(here + sign * offset(j) + ns, ns)

    def rows(j, count=1):
        return pl.ds(pl.multiple_of(j * TOKS, TOKS), count * TOKS)

    def lats(j, count=1):
        return pl.ds(pl.multiple_of(j * LAT, LAT), count * LAT)

    def to_seq(src, dst, send, recv, z):
        return pltpu.make_async_remote_copy(
            src_ref=src, dst_ref=dst, send_sem=send, recv_sem=recv,
            device_id={"seq": z}, device_id_type=pl.DeviceIdType.MESH)

    def to_frame(src, dst, send, recv, f):
        return pltpu.make_async_remote_copy(
            src_ref=src, dst_ref=dst, send_sem=send, recv_sem=recv,
            device_id={"frame": f}, device_id_type=pl.DeviceIdType.MESH)

    barrier = pltpu.get_barrier_semaphore()

    def greet(j, _):
        pl.semaphore_signal(barrier, inc=1, device_id={"seq": peer(j, 1)},
                            device_id_type=pl.DeviceIdType.MESH)
        return 0

    lax.fori_loop(1, ns, greet, 0)
    for f in (after, before):
        pl.semaphore_signal(barrier, inc=1, device_id={"frame": f},
                            device_id_type=pl.DeviceIdType.MESH)

    def columns(h):
        return pl.ds(pl.multiple_of(h * HD, HD), HD)

    own_q = pltpu.make_async_copy(q_hbm.at[0, :, columns(here)], qbuf.at[rows(0)], own_sem.at[0])
    own_k = pltpu.make_async_copy(k_hbm.at[0, :, columns(here)], keys.at[rows(0)], own_sem.at[1])
    own_q.start()
    own_k.start()

    for h in range(ns):
        part = jnp.dot(v_ref[0, :, h * HD:(h + 1) * HD], w_ref[h * HD:(h + 1) * HD, :],
                       preferred_element_type=F32)
        vsend[h * LAT:(h + 1) * LAT, :] = part.T.astype(BF16)

    pl.semaphore_wait(barrier, ns + 1)

    def send_k(j, _):
        z = peer(j, 1)
        to_seq(k_hbm.at[0, :, columns(z)], keys.at[rows(j)], k_out, k_in.at[j], z).start()
        return 0

    def send_v(j, _):
        z = peer(j, 1)
        to_seq(vsend.at[lats(z)], vals.at[lats(j)], v_out, v_in.at[j], z).start()
        return 0

    def send_q(j, _):
        z = peer(j, 1)
        to_seq(q_hbm.at[0, :, columns(z)], qbuf.at[rows(j)], q_out, q_in.at[j], z).start()
        return 0

    lax.fori_loop(1, ns, send_k, 0)
    lax.fori_loop(1, ns, send_v, 0)
    lax.fori_loop(1, ns, send_q, 0)
    vals[0:LAT, :] = vsend[lats(here), :]
    own_k.wait()
    own_q.wait()

    def arrived(j, _):
        to_seq(keys.at[rows(j)], keys.at[rows(j)], k_out, k_in.at[j], here).wait_recv()
        to_seq(vals.at[lats(j)], vals.at[lats(j)], v_out, v_in.at[j], here).wait_recv()
        return 0

    def forwards(g, side):
        f = (after, before)[side]
        slot = 1 + side
        return (
            to_frame(keys.at[rows(g * per, per)], keys.at[rows(slot * ns + g * per, per)],
                     f_out.at[2 * side], f_in.at[2 * side, g], f),
            to_frame(vals.at[lats(g * per, per)], vals.at[lats(slot * ns + g * per, per)],
                     f_out.at[2 * side + 1], f_in.at[2 * side + 1, g], f),
        )

    for g in range(GROUPS):
        lax.fori_loop(max(1, g * per), (g + 1) * per, arrived, 0)
        for side in range(2):
            for copy in forwards(g, side):
                copy.start()

    level = jnp.full((8, TOKS), time_ref[0], jnp.int32).astype(F32)
    step_size = (sigma_of(level - 1.0) - sigma_of(level))[0:1, :]
    latent_t = latent_ref[0].T

    weighted[LAT:, 0:toks] = jnp.ones((SUMS, toks), BF16)
    for j in range(ns):
        weighted[0:LAT, j * TOKS:(j + 1) * TOKS] = vals[j * LAT:(j + 1) * LAT, :]

    has = (
        jnp.where(jnp.logical_and(back_ref[0] >= 1, place >= 1), 1.0, 0.0),
        jnp.where(jnp.logical_and(ahead_ref[0] >= 1, place <= nf - 2), 1.0, 0.0),
    )
    for side in range(2):
        slot = 1 + side
        for g in range(GROUPS):
            for copy in forwards(g, side):
                copy.wait_recv()
        yes = jnp.full((TOKS, TOKS), has[side], F32)
        no = (1.0 - yes).astype(BF16)
        yes = yes.astype(BF16)
        weighted[LAT:, slot * toks:(slot + 1) * toks] = jnp.full((SUMS, toks), has[side], F32).astype(BF16)
        for j in range(ns):
            k = slot * ns + j
            keys[k * TOKS:(k + 1) * TOKS, :] = (
                keys[k * TOKS:(k + 1) * TOKS, :] * yes + keys[j * TOKS:(j + 1) * TOKS, :] * no)
            weighted[0:LAT, k * TOKS:(k + 1) * TOKS] = vals[k * LAT:(k + 1) * LAT, :] * yes[0:LAT]

    chunks = 3 * toks // CHUNK
    blocks = ns // 2

    def wait_q(b):
        for j in (2 * b, 2 * b + 1):
            copy = to_seq(qbuf.at[rows(j)], qbuf.at[rows(j)], q_out, q_in.at[j], here)
            if isinstance(j, int):
                if j > 0:
                    copy.wait_recv()
            else:
                copy.wait_recv()
        return qbuf[pl.ds(pl.multiple_of(b * PAIR, PAIR), PAIR), :]

    def score(q, c, held, top):
        s = lax.dot_general(keys[c * CHUNK:(c + 1) * CHUNK, :], q, (((1,), (1,)), ((), ())),
                            preferred_element_type=F32)
        held[c * CHUNK:(c + 1) * CHUNK, :] = s
        t = jnp.max(s.reshape(CHUNK // 8, 8, PAIR), axis=0)
        return t if top is None else jnp.maximum(top, t)

    def gather(m, c, held, acc):
        p = jnp.exp2(held[c * CHUNK:(c + 1) * CHUNK, :] * RATE - m).astype(BF16)
        r = jnp.dot(weighted[:, c * CHUNK:(c + 1) * CHUNK], p, preferred_element_type=F32)
        return r if acc is None else acc + r

    def finish(b, acc):
        out = (acc[0:LAT] / acc[LAT:LAT + 1]).astype(BF16)
        for i in range(2):
            j = 2 * b + i
            osend[lats(j), :] = out[:, i * TOKS:(i + 1) * TOKS]
            z = peer(j, -1)
            copy = to_seq(osend.at[lats(j)], obuf.at[lats(j)], o_out, o_in.at[j], z)
            if i == 1:
                copy.start()
            else:
                @pl.when(j > 0)
                def _():
                    copy.start()

    def peak(top):
        return jnp.max(top, axis=0, keepdims=True) * RATE

    def both(b_next, held_next, b, m, held):
        q = wait_q(b_next)
        top = acc = None
        for c in range(chunks):
            top = score(q, c, held_next, top)
            acc = gather(m, c, held, acc)
        finish(b, acc)
        return peak(top)

    q = wait_q(0)
    top = None
    for c in range(chunks):
        top = score(q, c, s0, top)
    m = peak(top)

    def two(i, m):
        m = both(2 * i + 1, s1, 2 * i, m, s0)
        return both(2 * i + 2, s0, 2 * i + 1, m, s1)

    m = lax.fori_loop(0, blocks // 2 - 1, two, m)
    m = both(blocks - 1, s1, blocks - 2, m, s0)
    acc = None
    for c in range(chunks):
        acc = gather(m, c, s1, acc)
    finish(blocks - 1, acc)

    def add(j, total):
        to_seq(obuf.at[lats(j)], obuf.at[lats(j)], o_out, o_in.at[j], here).wait_recv()
        return total + obuf[lats(j), :].astype(F32)

    total = lax.fori_loop(1, ns, add, osend[0:LAT, :].astype(F32))
    mine[...] = latent_t + step_size * total
    pass_on = to_frame(mine, theirs, m_sems.at[0], m_sems.at[1], before)
    pass_on.start()
    vel_ref[0] = total.T

    rest = pl.ds(TOKS, (ns - 1) * TOKS)
    rest_lat = pl.ds(LAT, (ns - 1) * LAT)
    to_seq(keys.at[rest], keys.at[rest], k_out, k_in.at[0], here).wait_send()
    to_seq(vals.at[rest_lat], vals.at[rest_lat], v_out, v_in.at[0], here).wait_send()
    to_seq(qbuf.at[rest], qbuf.at[rest], q_out, q_in.at[0], here).wait_send()
    to_seq(osend.at[rest_lat], osend.at[rest_lat], o_out, o_in.at[0], here).wait_send()
    for side in range(2):
        whole = pl.ds(0, toks)
        whole_lat = pl.ds(0, ns * LAT)
        to_frame(keys.at[whole], keys.at[whole], f_out.at[2 * side], f_in.at[0, 0], place).wait_send()
        to_frame(vals.at[whole_lat], vals.at[whole_lat], f_out.at[2 * side + 1], f_in.at[0, 0], place).wait_send()
    pass_on.wait()
    last = jnp.full((TOKS, LAT), place, jnp.int32) == nf - 1
    new_ref[0] = jnp.where(last, noise_ref[...], theirs[...].T)


def on_device(nf, ns, queries, key_proj, values, back_count, ahead_count, timestep, latent, noise_frame, w_final):
    smem = pl.BlockSpec(memory_space=pltpu.SMEM)
    vmem = pl.BlockSpec(memory_space=pltpu.VMEM)
    anywhere = pl.BlockSpec(memory_space=pl.ANY)
    toks = ns * TOKS
    dma = pltpu.SemaphoreType.DMA
    out = jax.ShapeDtypeStruct((1, TOKS, LAT), F32)
    pairs = 2 * toks * 3 * toks
    return pl.pallas_call(
        functools.partial(kernel, ns, nf),
        out_shape=(out, out),
        in_specs=[smem, smem, smem, anywhere, anywhere, vmem, vmem, vmem, vmem],
        out_specs=(vmem, vmem),
        scratch_shapes=[
            pltpu.VMEM((3 * toks, HD), BF16),
            pltpu.VMEM((3 * ns * LAT, TOKS), BF16),
            pltpu.VMEM((ns * LAT, TOKS), BF16),
            pltpu.VMEM((LAT + SUMS, 3 * toks), BF16),
            pltpu.VMEM((toks, HD), BF16),
            pltpu.VMEM((ns * LAT, TOKS), BF16),
            pltpu.VMEM((ns * LAT, TOKS), BF16),
            pltpu.VMEM((LAT, TOKS), F32),
            pltpu.VMEM((LAT, TOKS), F32),
            pltpu.VMEM((3 * toks, PAIR), F32),
            pltpu.VMEM((3 * toks, PAIR), F32),
            dma((2,)), dma, dma, dma, dma, dma((4,)), dma((2,)),
            dma((ns,)), dma((ns,)), dma((ns,)), dma((ns,)), dma((4, GROUPS)),
        ],
        compiler_params=pltpu.CompilerParams(
            collective_id=0, has_side_effects=True, vmem_limit_bytes=48 << 20),
        cost_estimate=pl.CostEstimate(
            flops=pairs * (HD + LAT), bytes_accessed=4 << 20, transcendentals=pairs // 2),
    )(back_count, ahead_count, timestep, queries, key_proj, values, w_final, latent, noise_frame)


def solution(mesh):
    nf, ns = mesh.shape["frame"], mesh.shape["seq"]
    spread = P("frame", "seq", None)
    placed = (spread, spread, spread, P("frame"), P("frame"), P("frame"), spread, P("seq", None), P())
    return jax.shard_map(
        functools.partial(on_device, nf, ns),
        mesh=mesh,
        in_specs=placed,
        out_specs=(spread, spread),
        check_vma=False,
    )
```

```python
import functools
import math

import jax
import jax.numpy as jnp
from jax import lax
from jax.experimental import pallas as pl
from jax.experimental.pallas import tpu as pltpu
from jax.sharding import PartitionSpec as P

HD = 128
TOKS = 128
LAT = 64
STEPS = 50
SHIFT = 7.0
RATE = HD ** (-0.5) * math.log2(math.e)
F32, BF16 = jnp.float32, jnp.bfloat16
CHUNK = 256
PAIR = 2 * TOKS
SUMS = 16
GROUPS = 4
HOPS = ()


def sigma_of(index):
    share = index / STEPS
    return SHIFT * share / (1.0 + (SHIFT - 1.0) * share)


def kernel(
    ns, nf, back_hbm, ahead_hbm, time_hbm, q_hbm, k_hbm, v_hbm, w_hbm, latent_hbm, noise_hbm,
    vel_ref, new_ref,
    back_ref, ahead_ref, time_ref, v_ref, w_ref, latent_ref, noise_ref, keys, vals, vsend, weighted, qbuf, osend, obuf, hsend, hbuf, mine, theirs, s0, s1,
    own_sem, k_out, v_out, q_out, o_out, h_out, f_out, m_sems, k_in, v_in, q_in, o_in, h_in, f_in,
):
    place, here = lax.axis_index("frame"), lax.axis_index("seq")
    after, before = lax.rem(place + 1, nf), lax.rem(place + nf - 1, nf)
    half = ns // 2
    per = ns // GROUPS
    toks = ns * TOKS

    def offset(j):
        return jnp.where(j == 0, 0, jnp.where(j % 2 == 0, half - j // 2, (j - 1) // 2 - half))

    def peer(j, sign):
        return lax.rem(here + sign * offset(j) + ns, ns)

    def rows(j, count=1):
        return pl.ds(pl.multiple_of(j * TOKS, TOKS), count * TOKS)

    def lats(j, count=1):
        return pl.ds(pl.multiple_of(j * LAT, LAT), count * LAT)

    def to_seq(src, dst, send, recv, z):
        return pltpu.make_async_remote_copy(
            src_ref=src, dst_ref=dst, send_sem=send, recv_sem=recv,
            device_id={"seq": z}, device_id_type=pl.DeviceIdType.MESH)

    def to_frame(src, dst, send, recv, f):
        return pltpu.make_async_remote_copy(
            src_ref=src, dst_ref=dst, send_sem=send, recv_sem=recv,
            device_id={"frame": f}, device_id_type=pl.DeviceIdType.MESH)

    barrier = pltpu.get_barrier_semaphore()

    def greet(j, _):
        pl.semaphore_signal(barrier, inc=1, device_id={"seq": peer(j, 1)},
                            device_id_type=pl.DeviceIdType.MESH)
        return 0

    lax.fori_loop(1, ns, greet, 0)
    for f in (after, before):
        pl.semaphore_signal(barrier, inc=1, device_id={"frame": f},
                            device_id_type=pl.DeviceIdType.MESH)

    def columns(h):
        return pl.ds(pl.multiple_of(h * HD, HD), HD)

    own_v = pltpu.make_async_copy(v_hbm.at[0], v_ref, own_sem.at[2])
    own_w = pltpu.make_async_copy(w_hbm, w_ref, own_sem.at[3])
    own_latent = pltpu.make_async_copy(latent_hbm.at[0], latent_ref, own_sem.at[4])
    own_noise = pltpu.make_async_copy(noise_hbm, noise_ref, own_sem.at[5])
    scalars = [
        pltpu.make_async_copy(src, dst, own_sem.at[6 + i])
        for i, (src, dst) in enumerate(((back_hbm, back_ref), (ahead_hbm, ahead_ref), (time_hbm, time_ref)))
    ]
    own_q = pltpu.make_async_copy(q_hbm.at[0, :, columns(here)], qbuf.at[rows(0)], own_sem.at[0])
    own_k = pltpu.make_async_copy(k_hbm.at[0, :, columns(here)], keys.at[rows(0)], own_sem.at[1])
    for copy in (own_v, own_w, own_k, own_q, own_latent, own_noise, *scalars):
        copy.start()

    pl.semaphore_wait(barrier, ns + 1)

    def send_k(j, _):
        z = peer(j, 1)
        to_seq(k_hbm.at[0, :, columns(z)], keys.at[rows(j)], k_out, k_in.at[j], z).start()
        return 0

    def send_v(j, _):
        z = peer(j, 1)
        to_seq(vsend.at[lats(z)], vals.at[lats(j)], v_out, v_in.at[j], z).start()
        return 0

    def send_q(j, _):
        z = peer(j, 1)
        to_seq(q_hbm.at[0, :, columns(z)], qbuf.at[rows(j)], q_out, q_in.at[j], z).start()
        return 0

    lax.fori_loop(1, per, send_k, 0)
    own_v.wait()
    own_w.wait()
    for h in range(ns):
        part = lax.dot_general(w_ref[:, h * HD:(h + 1) * HD], v_ref[:, h * HD:(h + 1) * HD],
                               (((1,), (1,)), ((), ())), preferred_element_type=F32)
        vsend[h * LAT:(h + 1) * LAT, :] = part.astype(BF16)

    lax.fori_loop(1, per, send_v, 0)
    lax.fori_loop(per, ns, send_k, 0)
    lax.fori_loop(per, ns, send_v, 0)
    lax.fori_loop(1, ns, send_q, 0)
    vals[0:LAT, :] = vsend[lats(here), :]
    own_k.wait()
    own_q.wait()
    own_latent.wait()
    own_noise.wait()
    for copy in scalars:
        copy.wait()

    def arrived(j, _):
        to_seq(keys.at[rows(j)], keys.at[rows(j)], k_out, k_in.at[j], here).wait_recv()
        to_seq(vals.at[lats(j)], vals.at[lats(j)], v_out, v_in.at[j], here).wait_recv()
        return 0

    def forwards(g, side):
        f = (after, before)[side]
        slot = 1 + side
        return (
            to_frame(keys.at[rows(g * per, per)], keys.at[rows(slot * ns + g * per, per)],
                     f_out.at[2 * side], f_in.at[2 * side, g], f),
            to_frame(vals.at[lats(g * per, per)], vals.at[lats(slot * ns + g * per, per)],
                     f_out.at[2 * side + 1], f_in.at[2 * side + 1, g], f),
        )

    for g in range(GROUPS):
        lax.fori_loop(max(1, g * per), (g + 1) * per, arrived, 0)
        for side in range(2):
            for copy in forwards(g, side):
                copy.start()

    level = jnp.full((8, TOKS), time_ref[0], jnp.int32).astype(F32)
    step_size = (sigma_of(level - 1.0) - sigma_of(level))[0:1, :]
    latent_t = latent_ref[...]

    weighted[LAT:, 0:toks] = jnp.ones((SUMS, toks), BF16)
    for j in range(ns):
        weighted[0:LAT, j * TOKS:(j + 1) * TOKS] = vals[j * LAT:(j + 1) * LAT, :]

    has = (
        jnp.where(jnp.logical_and(back_ref[0] >= 1, place >= 1), 1.0, 0.0),
        jnp.where(jnp.logical_and(ahead_ref[0] >= 1, place <= nf - 2), 1.0, 0.0),
    )
    for side in range(2):
        slot = 1 + side
        for g in range(GROUPS):
            for copy in forwards(g, side):
                copy.wait_recv()
        yes = jnp.full((TOKS, TOKS), has[side], F32)
        no = (1.0 - yes).astype(BF16)
        yes = yes.astype(BF16)
        weighted[LAT:, slot * toks:(slot + 1) * toks] = jnp.full((SUMS, toks), has[side], F32).astype(BF16)
        for j in range(ns):
            k = slot * ns + j
            keys[k * TOKS:(k + 1) * TOKS, :] = (
                keys[k * TOKS:(k + 1) * TOKS, :] * yes + keys[j * TOKS:(j + 1) * TOKS, :] * no)
            weighted[0:LAT, k * TOKS:(k + 1) * TOKS] = vals[k * LAT:(k + 1) * LAT, :] * yes[0:LAT]

    chunks = 3 * toks // CHUNK
    blocks = ns // 2

    def hops(d, i):
        return d in HOPS and d <= half - 1 + i

    def gets(d, i):
        return hops(d + 1, i)

    def wait_q(b):
        for j in (2 * b, 2 * b + 1):
            if not isinstance(j, int) or j > 0:
                to_seq(qbuf.at[rows(j)], qbuf.at[rows(j)], q_out, q_in.at[j], here).wait_recv()
        return qbuf[pl.ds(pl.multiple_of(b * PAIR, PAIR), PAIR), :]

    def score(q, c, held, top):
        s = lax.dot_general(keys[c * CHUNK:(c + 1) * CHUNK, :], q, (((1,), (1,)), ((), ())),
                            preferred_element_type=F32)
        held[c * CHUNK:(c + 1) * CHUNK, :] = s
        t = jnp.max(s.reshape(CHUNK // 8, 8, PAIR), axis=0)
        return t if top is None else jnp.maximum(top, t)

    def gather(m, c, held, acc):
        p = jnp.exp2(held[c * CHUNK:(c + 1) * CHUNK, :] * RATE - m).astype(BF16)
        r = jnp.dot(weighted[:, c * CHUNK:(c + 1) * CHUNK], p, preferred_element_type=F32)
        return r if acc is None else acc + r

    def step_on(j, i):
        z = lax.rem(here + (1 if i else ns - 1), ns)
        return to_seq(hsend.at[lats(j)], hbuf.at[lats(j + 2)], h_out.at[j], h_in.at[j + 2], z)

    def straight(j):
        return to_seq(osend.at[lats(j)], obuf.at[lats(j)], o_out.at[j], o_in.at[j], peer(j, -1))

    def finish(b, acc):
        out = acc[0:LAT] / acc[LAT:LAT + 1]
        for i in range(2):
            j = 2 * b + i
            mine_now = out[:, i * TOKS:(i + 1) * TOKS]
            if isinstance(b, int):
                if gets(half - b, i):
                    step_on(j - 2, i).wait_recv()
                    mine_now = mine_now + hbuf[lats(j), :]
                if hops(half - b, i):
                    hsend[lats(j), :] = mine_now
                    step_on(j, i).start()
                else:
                    osend[lats(j), :] = mine_now.astype(BF16)
                    straight(j).start()
            else:
                given, stepped, own = (
                    functools.reduce(jnp.logical_or, [b == half - d for d in range(1, half + 1) if test(d, i)], False)
                    for test in (gets, hops, lambda d, i: d == half and i == 0))
                hsend[lats(j), :] = mine_now

                @pl.when(given)
                def _():
                    step_on(j - 2, i).wait_recv()
                    hsend[lats(j), :] = hsend[lats(j), :] + hbuf[lats(j), :]

                @pl.when(stepped)
                def _():
                    step_on(j, i).start()

                @pl.when(jnp.logical_not(jnp.logical_or(stepped, own)))
                def _():
                    osend[lats(j), :] = hsend[lats(j), :].astype(BF16)
                    straight(j).start()

    def peak(top):
        return jnp.max(top, axis=0, keepdims=True) * RATE

    def both(b_next, held_next, b, m, held):
        q = wait_q(b_next)
        top = acc = None
        for c in range(chunks):
            top = score(q, c, held_next, top)
            acc = gather(m, c, held, acc)
        finish(b, acc)
        return peak(top)

    q = wait_q(0)
    top = None
    for c in range(chunks):
        top = score(q, c, s0, top)
    m = peak(top)

    def two(i, m):
        m = both(2 * i + 1, s1, 2 * i, m, s0)
        return both(2 * i + 2, s0, 2 * i + 1, m, s1)

    m = lax.fori_loop(0, blocks // 2 - 1, two, m)
    m = both(blocks - 1, s1, blocks - 2, m, s0)
    acc = None
    for c in range(chunks):
        acc = gather(m, c, s1, acc)
    finish(blocks - 1, acc)

    total = hsend[0:LAT, :]
    for j in range(1, ns):
        if not hops(half - j // 2, j % 2):
            straight(j).wait_recv()
            total = total + obuf[j * LAT:(j + 1) * LAT, :].astype(F32)
    mine[...] = latent_t + step_size * total
    pass_on = to_frame(mine, theirs, m_sems.at[0], m_sems.at[1], before)
    pass_on.start()
    vel_ref[0] = total

    rest = pl.ds(TOKS, (ns - 1) * TOKS)
    rest_lat = pl.ds(LAT, (ns - 1) * LAT)
    to_seq(keys.at[rest], keys.at[rest], k_out, k_in.at[0], here).wait_send()
    to_seq(vals.at[rest_lat], vals.at[rest_lat], v_out, v_in.at[0], here).wait_send()
    to_seq(qbuf.at[rest], qbuf.at[rest], q_out, q_in.at[0], here).wait_send()
    for j in range(1, ns):
        if hops(half - j // 2, j % 2):
            step_on(j, j % 2).wait_send()
        else:
            straight(j).wait_send()
    for side in range(2):
        whole = pl.ds(0, toks)
        whole_lat = pl.ds(0, ns * LAT)
        to_frame(keys.at[whole], keys.at[whole], f_out.at[2 * side], f_in.at[0, 0], place).wait_send()
        to_frame(vals.at[whole_lat], vals.at[whole_lat], f_out.at[2 * side + 1], f_in.at[0, 0], place).wait_send()
    pass_on.wait()
    last = jnp.full((LAT, TOKS), place, jnp.int32) == nf - 1
    new_ref[0] = jnp.where(last, noise_ref[...], theirs[...])


def on_device(nf, ns, queries, key_proj, values, back_count, ahead_count, timestep, latent, noise_frame, w_final):
    vmem = pl.BlockSpec(memory_space=pltpu.VMEM)
    anywhere = pl.BlockSpec(memory_space=pltpu.HBM)
    toks = ns * TOKS
    dma = pltpu.SemaphoreType.DMA
    out = jax.ShapeDtypeStruct((1, LAT, TOKS), F32)
    pairs = 2 * toks * 3 * toks
    velocity, new_queue = pl.pallas_call(
        functools.partial(kernel, ns, nf),
        out_shape=(out, out),
        in_specs=[anywhere] * 9,
        out_specs=(vmem, vmem),
        scratch_shapes=[
            pltpu.SMEM((1,), jnp.int32),
            pltpu.SMEM((1,), jnp.int32),
            pltpu.SMEM((1,), jnp.int32),
            pltpu.VMEM((TOKS, ns * HD), BF16),
            pltpu.VMEM((LAT, ns * HD), BF16),
            pltpu.VMEM((LAT, TOKS), F32),
            pltpu.VMEM((LAT, TOKS), F32),
            pltpu.VMEM((3 * toks, HD), BF16),
            pltpu.VMEM((3 * ns * LAT, TOKS), BF16),
            pltpu.VMEM((ns * LAT, TOKS), BF16),
            pltpu.VMEM((LAT + SUMS, 3 * toks), BF16),
            pltpu.VMEM((toks, HD), BF16),
            pltpu.VMEM((ns * LAT, TOKS), BF16),
            pltpu.VMEM((ns * LAT, TOKS), BF16),
            pltpu.VMEM((ns * LAT, TOKS), F32),
            pltpu.VMEM((ns * LAT, TOKS), F32),
            pltpu.VMEM((LAT, TOKS), F32),
            pltpu.VMEM((LAT, TOKS), F32),
            pltpu.VMEM((3 * toks, PAIR), F32),
            pltpu.VMEM((3 * toks, PAIR), F32),
            dma((9,)), dma, dma, dma, dma((ns,)), dma((ns,)), dma((4,)), dma((2,)),
            dma((ns,)), dma((ns,)), dma((ns,)), dma((ns,)), dma((ns,)), dma((4, GROUPS)),
        ],
        compiler_params=pltpu.CompilerParams(
            collective_id=0, has_side_effects=True, vmem_limit_bytes=(64 << 20) - (400 << 10)),
        cost_estimate=pl.CostEstimate(
            flops=pairs * (HD + LAT), bytes_accessed=4 << 20, transcendentals=pairs // 2),
    )(back_count, ahead_count, timestep, queries, key_proj, values,
      w_final.T, jnp.swapaxes(latent, 1, 2), noise_frame.T)
    return jnp.swapaxes(velocity, 1, 2), jnp.swapaxes(new_queue, 1, 2)


def solution(mesh):
    nf, ns = mesh.shape["frame"], mesh.shape["seq"]
    spread = P("frame", "seq", None)
    placed = (spread, spread, spread, P("frame"), P("frame"), P("frame"), spread, P("seq", None), P())
    return jax.shard_map(
        functools.partial(on_device, nf, ns),
        mesh=mesh,
        in_specs=placed,
        out_specs=(spread, spread),
        check_vma=False,
    )
```

```python
import functools
import math

import jax
import jax.numpy as jnp
from jax import lax
from jax.experimental import pallas as pl
from jax.experimental.pallas import tpu as pltpu
from jax.sharding import PartitionSpec as P

HD = 128
TOKS = 128
LAT = 64
STEPS = 50
SHIFT = 7.0
RATE = HD ** (-0.5) * math.log2(math.e)
F32, BF16 = jnp.float32, jnp.bfloat16
CHUNK = 256
PAIR = 2 * TOKS
SUMS = 16
GROUPS = 4


def sigma_of(index):
    share = index / STEPS
    return SHIFT * share / (1.0 + (SHIFT - 1.0) * share)


def kernel(
    ns, nf, back_hbm, ahead_hbm, time_hbm, q_hbm, k_hbm, v_hbm, w_hbm, latent_hbm,
    vel_hbm, new_hbm,
    back_ref, ahead_ref, time_ref, v_ref, w_ref, latent_ref, vel_ref,
    keys, vals, vsend, weighted, qbuf, osend, obuf, own, mine, s0, s1,
    own_sem, k_out, v_out, q_out, o_out, f_out, m_sems, k_in, v_in, q_in, o_in, f_in,
):
    place, here = lax.axis_index("frame"), lax.axis_index("seq")
    after, before = lax.rem(place + 1, nf), lax.rem(place + nf - 1, nf)
    half = ns // 2
    per = ns // GROUPS
    toks = ns * TOKS

    def offset(j):
        return jnp.where(j == 0, 0, jnp.where(j % 2 == 0, half - j // 2, (j - 1) // 2 - half))

    def ring(z):
        return lax.rem(z + ns, ns)

    def owner(j):
        return ring(here - offset(j))

    def rows(j, count=1):
        return pl.ds(pl.multiple_of(j * TOKS, TOKS), count * TOKS)

    def lats(j, count=1):
        return pl.ds(pl.multiple_of(j * LAT, LAT), count * LAT)

    def to_seq(src, dst, send, recv, z):
        return pltpu.make_async_remote_copy(
            src_ref=src, dst_ref=dst, send_sem=send, recv_sem=recv,
            device_id={"seq": z}, device_id_type=pl.DeviceIdType.MESH)

    def to_frame(src, dst, send, recv, f):
        return pltpu.make_async_remote_copy(
            src_ref=src, dst_ref=dst, send_sem=send, recv_sem=recv,
            device_id={"frame": f}, device_id_type=pl.DeviceIdType.MESH)

    barrier = pltpu.get_barrier_semaphore()

    def greet(j, _):
        pl.semaphore_signal(barrier, inc=1, device_id={"seq": ring(here + j)},
                            device_id_type=pl.DeviceIdType.MESH)
        return 0

    lax.fori_loop(1, ns, greet, 0)
    for f in (after, before):
        pl.semaphore_signal(barrier, inc=1, device_id={"frame": f},
                            device_id_type=pl.DeviceIdType.MESH)

    def columns(h):
        return pl.ds(pl.multiple_of(h * HD, HD), HD)

    own_v = pltpu.make_async_copy(v_hbm.at[0], v_ref, own_sem.at[2])
    own_w = pltpu.make_async_copy(w_hbm, w_ref, own_sem.at[3])
    own_latent = pltpu.make_async_copy(latent_hbm.at[0], latent_ref, own_sem.at[4])
    out_vel = pltpu.make_async_copy(vel_ref, vel_hbm.at[0], own_sem.at[5])
    scalars = [
        pltpu.make_async_copy(src, dst, own_sem.at[6 + i])
        for i, (src, dst) in enumerate(((back_hbm, back_ref), (ahead_hbm, ahead_ref), (time_hbm, time_ref)))
    ]
    own_q = pltpu.make_async_copy(q_hbm.at[0, :, columns(here)], qbuf.at[rows(0)], own_sem.at[0])
    own_k = pltpu.make_async_copy(k_hbm.at[0, :, columns(here)], keys.at[rows(0)], own_sem.at[1])
    for copy in (own_v, own_w, own_k, own_q, own_latent, *scalars):
        copy.start()

    pl.semaphore_wait(barrier, ns + 1)

    def send_k(j, _):
        z = ring(here + offset(j))
        to_seq(k_hbm.at[0, :, columns(z)], keys.at[rows(j)], k_out, k_in.at[j], z).start()
        return 0

    def send_v(j, _):
        z = ring(here + offset(j))
        to_seq(vsend.at[lats(z)], vals.at[lats(j)], v_out, v_in.at[j], z).start()
        return 0

    def send_q(j, _):
        z = ring(here + offset(j))
        to_seq(q_hbm.at[0, :, columns(z)], qbuf.at[rows(j)], q_out, q_in.at[j], z).start()
        return 0

    lax.fori_loop(1, per, send_k, 0)
    own_v.wait()
    own_w.wait()
    for h in range(ns):
        part = lax.dot_general(w_ref[:, h * HD:(h + 1) * HD], v_ref[:, h * HD:(h + 1) * HD],
                               (((1,), (1,)), ((), ())), preferred_element_type=F32)
        vsend[h * LAT:(h + 1) * LAT, :] = part.astype(BF16)

    lax.fori_loop(1, per, send_v, 0)
    lax.fori_loop(per, ns, send_k, 0)
    lax.fori_loop(per, ns, send_v, 0)
    lax.fori_loop(1, ns, send_q, 0)
    vals[0:LAT, :] = vsend[lats(here), :]
    own_k.wait()
    own_q.wait()
    own_latent.wait()
    for copy in scalars:
        copy.wait()

    def arrived(j, _):
        to_seq(keys.at[rows(j)], keys.at[rows(j)], k_out, k_in.at[j], here).wait_recv()
        to_seq(vals.at[lats(j)], vals.at[lats(j)], v_out, v_in.at[j], here).wait_recv()
        return 0

    def forwards(g, side):
        f = (after, before)[side]
        slot = 1 + side
        return (
            to_frame(keys.at[rows(g * per, per)], keys.at[rows(slot * ns + g * per, per)],
                     f_out.at[2 * side], f_in.at[2 * side, g], f),
            to_frame(vals.at[lats(g * per, per)], vals.at[lats(slot * ns + g * per, per)],
                     f_out.at[2 * side + 1], f_in.at[2 * side + 1, g], f),
        )

    for g in range(GROUPS):
        lax.fori_loop(max(1, g * per), (g + 1) * per, arrived, 0)
        for side in range(2):
            for copy in forwards(g, side):
                copy.start()

    level = jnp.full((8, TOKS), time_ref[0], jnp.int32).astype(F32)
    step_size = (sigma_of(level - 1.0) - sigma_of(level))[0:1, :]
    latent_t = latent_ref[...]

    weighted[LAT:, 0:toks] = jnp.ones((SUMS, toks), BF16)
    for j in range(ns):
        weighted[0:LAT, j * TOKS:(j + 1) * TOKS] = vals[j * LAT:(j + 1) * LAT, :]

    has = (
        jnp.where(jnp.logical_and(back_ref[0] >= 1, place >= 1), 1.0, 0.0),
        jnp.where(jnp.logical_and(ahead_ref[0] >= 1, place <= nf - 2), 1.0, 0.0),
    )
    for side in range(2):
        slot = 1 + side
        for g in range(GROUPS):
            for copy in forwards(g, side):
                copy.wait_recv()
        yes = jnp.full((TOKS, TOKS), has[side], F32)
        no = (1.0 - yes).astype(BF16)
        yes = yes.astype(BF16)
        weighted[LAT:, slot * toks:(slot + 1) * toks] = jnp.full((SUMS, toks), has[side], F32).astype(BF16)
        for j in range(ns):
            k = slot * ns + j
            keys[k * TOKS:(k + 1) * TOKS, :] = (
                keys[k * TOKS:(k + 1) * TOKS, :] * yes + keys[j * TOKS:(j + 1) * TOKS, :] * no)
            weighted[0:LAT, k * TOKS:(k + 1) * TOKS] = vals[k * LAT:(k + 1) * LAT, :] * yes[0:LAT]

    chunks = 3 * toks // CHUNK
    blocks = ns // 2

    def wait_q(b):
        for j in (2 * b, 2 * b + 1):
            if not isinstance(j, int) or j > 0:
                to_seq(qbuf.at[rows(j)], qbuf.at[rows(j)], q_out, q_in.at[j], here).wait_recv()
        return qbuf[pl.ds(pl.multiple_of(b * PAIR, PAIR), PAIR), :]

    def score(q, c, held, top):
        s = lax.dot_general(keys[c * CHUNK:(c + 1) * CHUNK, :], q, (((1,), (1,)), ((), ())),
                            preferred_element_type=F32)
        held[c * CHUNK:(c + 1) * CHUNK, :] = s
        t = jnp.max(s.reshape(CHUNK // 8, 8, PAIR), axis=0)
        return t if top is None else jnp.maximum(top, t)

    def gather(m, c, held, acc):
        p = jnp.exp2(held[c * CHUNK:(c + 1) * CHUNK, :] * RATE - m).astype(BF16)
        r = jnp.dot(weighted[:, c * CHUNK:(c + 1) * CHUNK], p, preferred_element_type=F32)
        return r if acc is None else acc + r

    def straight(j):
        return to_seq(osend.at[lats(j)], obuf.at[lats(j)], o_out.at[j], o_in.at[j], owner(j))

    def finish(b, acc):
        out = acc[0:LAT] / acc[LAT:LAT + 1]
        for i in range(2):
            j = 2 * b + i
            part = out[:, i * TOKS:(i + 1) * TOKS]
            osend[lats(j), :] = part.astype(BF16)
            if i == 0:
                @pl.when(j == 0)
                def _():
                    own[...] = part

            @pl.when(j > 0)
            def _():
                straight(j).start()

    def peak(top):
        return jnp.max(top, axis=0, keepdims=True) * RATE

    def both(b_next, held_next, b, m, held):
        q = wait_q(b_next)
        top = acc = None
        for c in range(chunks):
            top = score(q, c, held_next, top)
            acc = gather(m, c, held, acc)
        finish(b, acc)
        return peak(top)

    q = wait_q(0)
    top = None
    for c in range(chunks):
        top = score(q, c, s0, top)
    m = peak(top)

    def two(i, m):
        m = both(2 * i + 1, s1, 2 * i, m, s0)
        return both(2 * i + 2, s0, 2 * i + 1, m, s1)

    m = lax.fori_loop(0, blocks // 2 - 1, two, m)
    m = both(blocks - 1, s1, blocks - 2, m, s0)
    acc = None
    for c in range(chunks):
        acc = gather(m, c, s1, acc)
    finish(blocks - 1, acc)

    total = own[...]
    for j in range(1, ns):
        to_seq(obuf.at[lats(j)], obuf.at[lats(j)], o_out.at[j], o_in.at[j], here).wait_recv()
        total = total + obuf[j * LAT:(j + 1) * LAT, :].astype(F32)
    mine[...] = latent_t + step_size * total
    pass_on = to_frame(mine, new_hbm.at[0], m_sems.at[0], m_sems.at[1], before)
    pass_on.start()
    vel_ref[...] = total
    out_vel.start()

    rest = pl.ds(TOKS, (ns - 1) * TOKS)
    rest_lat = pl.ds(LAT, (ns - 1) * LAT)
    to_seq(keys.at[rest], keys.at[rest], k_out, k_in.at[0], here).wait_send()
    to_seq(vals.at[rest_lat], vals.at[rest_lat], v_out, v_in.at[0], here).wait_send()
    to_seq(qbuf.at[rest], qbuf.at[rest], q_out, q_in.at[0], here).wait_send()
    for j in range(1, ns):
        to_seq(osend.at[lats(j)], osend.at[lats(j)], o_out.at[j], o_in.at[j], here).wait_send()
    for side in range(2):
        whole = pl.ds(0, toks)
        whole_lat = pl.ds(0, ns * LAT)
        to_frame(keys.at[whole], keys.at[whole], f_out.at[2 * side], f_in.at[0, 0], place).wait_send()
        to_frame(vals.at[whole_lat], vals.at[whole_lat], f_out.at[2 * side + 1], f_in.at[0, 0], place).wait_send()
    pass_on.wait()
    out_vel.wait()


def closing(nf, vel_ref, arrived_ref, noise_ref, vel_out, new_out):
    last = jnp.full((LAT, TOKS), lax.axis_index("frame"), jnp.int32) == nf - 1
    vel_out[...] = vel_ref[...]
    new_out[0] = jnp.where(last, noise_ref[...], arrived_ref[0])


def on_device(nf, ns, queries, key_proj, values, back_count, ahead_count, timestep, latent, noise_frame, w_final):
    anywhere = pl.BlockSpec(memory_space=pltpu.HBM)
    toks = ns * TOKS
    dma = pltpu.SemaphoreType.DMA
    out = jax.ShapeDtypeStruct((1, LAT, TOKS), F32)
    pairs = 2 * toks * 3 * toks
    velocity, arrived = pl.pallas_call(
        functools.partial(kernel, ns, nf),
        out_shape=(out, out),
        in_specs=[anywhere] * 8,
        out_specs=(anywhere, anywhere),
        scratch_shapes=[
            pltpu.SMEM((1,), jnp.int32),
            pltpu.SMEM((1,), jnp.int32),
            pltpu.SMEM((1,), jnp.int32),
            pltpu.VMEM((TOKS, ns * HD), BF16),
            pltpu.VMEM((LAT, ns * HD), BF16),
            pltpu.VMEM((LAT, TOKS), F32),
            pltpu.VMEM((LAT, TOKS), F32),
            pltpu.VMEM((3 * toks, HD), BF16),
            pltpu.VMEM((3 * ns * LAT, TOKS), BF16),
            pltpu.VMEM((ns * LAT, TOKS), BF16),
            pltpu.VMEM((LAT + SUMS, 3 * toks), BF16),
            pltpu.VMEM((toks, HD), BF16),
            pltpu.VMEM((ns * LAT, TOKS), BF16),
            pltpu.VMEM((ns * LAT, TOKS), BF16),
            pltpu.VMEM((LAT, TOKS), F32),
            pltpu.VMEM((LAT, TOKS), F32),
            pltpu.VMEM((3 * toks, PAIR), F32),
            pltpu.VMEM((3 * toks, PAIR), F32),
            dma((9,)), dma, dma, dma, dma((ns,)), dma((4,)), dma((2,)),
            dma((ns,)), dma((ns,)), dma((ns,)), dma((ns,)), dma((4, GROUPS)),
        ],
        compiler_params=pltpu.CompilerParams(
            collective_id=0, has_side_effects=True, vmem_limit_bytes=(64 << 20) - (400 << 10)),
        cost_estimate=pl.CostEstimate(
            flops=pairs * (HD + LAT), bytes_accessed=4 << 20, transcendentals=pairs // 2),
    )(back_count, ahead_count, timestep, queries, key_proj, values,
      w_final.T, jnp.swapaxes(latent, 1, 2))
    velocity, new_queue = pl.pallas_call(
        functools.partial(closing, nf),
        out_shape=(out, out),
        in_specs=[pl.BlockSpec(memory_space=pltpu.VMEM)] * 3,
        out_specs=(pl.BlockSpec(memory_space=pltpu.VMEM),) * 2,
    )(velocity, arrived, noise_frame.T)
    return jnp.swapaxes(velocity, 1, 2), jnp.swapaxes(new_queue, 1, 2)


def solution(mesh):
    nf, ns = mesh.shape["frame"], mesh.shape["seq"]
    spread = P("frame", "seq", None)
    placed = (spread, spread, spread, P("frame"), P("frame"), P("frame"), spread, P("seq", None), P())
    return jax.shard_map(
        functools.partial(on_device, nf, ns),
        mesh=mesh,
        in_specs=placed,
        out_specs=(spread, spread),
        check_vma=False,
    )
```

```python
import functools
import math

import jax
import jax.numpy as jnp
from jax import lax
from jax.experimental import pallas as pl
from jax.experimental.pallas import tpu as pltpu
from jax.sharding import PartitionSpec as P

HD = 128
TOKS = 128
LAT = 64
STEPS = 50
SHIFT = 7.0
RATE = HD ** (-0.5) * math.log2(math.e)
F32, BF16 = jnp.float32, jnp.bfloat16
CHUNK = 256
PAIR = 2 * TOKS
SUMS = 16
GROUPS = 4


def sigma_of(index):
    share = index / STEPS
    return SHIFT * share / (1.0 + (SHIFT - 1.0) * share)


def kernel(
    ns, nf, back_hbm, ahead_hbm, time_hbm, q_hbm, k_hbm, v_hbm, w_hbm, latent_hbm,
    vel_hbm, new_hbm,
    back_ref, ahead_ref, time_ref, v_ref, w_ref, latent_ref, vel_ref,
    keys, vals, vsend, weighted, qbuf, osend, obuf, own, mine, s0, s1,
    own_sem, k_out, v_out, q_out, o_out, f_out, m_sems, k_in, v_in, q_in, o_in, f_in,
):
    place, here = lax.axis_index("frame"), lax.axis_index("seq")
    after, before = lax.rem(place + 1, nf), lax.rem(place + nf - 1, nf)
    half = ns // 2
    per = ns // GROUPS
    toks = ns * TOKS

    def offset(j):
        return jnp.where(j == 0, 0, jnp.where(j % 2 == 0, half - j // 2, (j - 1) // 2 - half))

    def ring(z):
        return lax.rem(z + ns, ns)

    def owner(j):
        return ring(here - offset(j))

    def rows(j, count=1):
        return pl.ds(pl.multiple_of(j * TOKS, TOKS), count * TOKS)

    def lats(j, count=1):
        return pl.ds(pl.multiple_of(j * LAT, LAT), count * LAT)

    def to_seq(src, dst, send, recv, z):
        return pltpu.make_async_remote_copy(
            src_ref=src, dst_ref=dst, send_sem=send, recv_sem=recv,
            device_id={"seq": z}, device_id_type=pl.DeviceIdType.MESH)

    def to_frame(src, dst, send, recv, f):
        return pltpu.make_async_remote_copy(
            src_ref=src, dst_ref=dst, send_sem=send, recv_sem=recv,
            device_id={"frame": f}, device_id_type=pl.DeviceIdType.MESH)

    barrier = pltpu.get_barrier_semaphore()

    def greet(j, _):
        pl.semaphore_signal(barrier, inc=1, device_id={"seq": ring(here + j)},
                            device_id_type=pl.DeviceIdType.MESH)
        return 0

    lax.fori_loop(1, ns, greet, 0)
    for f in (after, before):
        pl.semaphore_signal(barrier, inc=1, device_id={"frame": f},
                            device_id_type=pl.DeviceIdType.MESH)

    def columns(h):
        return pl.ds(pl.multiple_of(h * HD, HD), HD)

    own_v = pltpu.make_async_copy(v_hbm.at[0], v_ref, own_sem.at[2])
    own_w = pltpu.make_async_copy(w_hbm, w_ref, own_sem.at[3])
    own_latent = pltpu.make_async_copy(latent_hbm.at[0], latent_ref, own_sem.at[4])
    out_vel = pltpu.make_async_copy(vel_ref, vel_hbm.at[0], own_sem.at[5])
    scalars = [
        pltpu.make_async_copy(src, dst, own_sem.at[6 + i])
        for i, (src, dst) in enumerate(((back_hbm, back_ref), (ahead_hbm, ahead_ref), (time_hbm, time_ref)))
    ]
    own_q = pltpu.make_async_copy(q_hbm.at[0, :, columns(here)], qbuf.at[rows(0)], own_sem.at[0])
    own_k = pltpu.make_async_copy(k_hbm.at[0, :, columns(here)], keys.at[rows(0)], own_sem.at[1])
    for copy in (own_v, own_w, own_k, own_q, own_latent, *scalars):
        copy.start()

    pl.semaphore_wait(barrier, ns + 1)

    def send_k(j, _):
        z = ring(here + offset(j))
        to_seq(k_hbm.at[0, :, columns(z)], keys.at[rows(j)], k_out, k_in.at[j], z).start()
        return 0

    def send_v(j, _):
        z = ring(here + offset(j))
        to_seq(vsend.at[lats(z)], vals.at[lats(j)], v_out, v_in.at[j], z).start()
        return 0

    def send_q(j, _):
        z = ring(here + offset(j))
        to_seq(q_hbm.at[0, :, columns(z)], qbuf.at[rows(j)], q_out, q_in.at[j], z).start()
        return 0

    lax.fori_loop(1, per, send_k, 0)
    own_v.wait()
    own_w.wait()
    for h in range(ns):
        part = lax.dot_general(w_ref[:, h * HD:(h + 1) * HD], v_ref[:, h * HD:(h + 1) * HD],
                               (((1,), (1,)), ((), ())), preferred_element_type=F32)
        vsend[h * LAT:(h + 1) * LAT, :] = part.astype(BF16)

    lax.fori_loop(1, per, send_v, 0)
    def send_kv(j, _):
        send_k(j, 0)
        send_v(j, 0)
        return 0

    lax.fori_loop(per, ns, send_kv, 0)
    lax.fori_loop(1, ns, send_q, 0)
    vals[0:LAT, :] = vsend[lats(here), :]
    own_k.wait()
    own_q.wait()
    own_latent.wait()
    for copy in scalars:
        copy.wait()

    def arrived(j, _):
        to_seq(keys.at[rows(j)], keys.at[rows(j)], k_out, k_in.at[j], here).wait_recv()
        to_seq(vals.at[lats(j)], vals.at[lats(j)], v_out, v_in.at[j], here).wait_recv()
        return 0

    def forwards(g, side):
        f = (after, before)[side]
        slot = 1 + side
        return (
            to_frame(keys.at[rows(g * per, per)], keys.at[rows(slot * ns + g * per, per)],
                     f_out.at[2 * side], f_in.at[2 * side, g], f),
            to_frame(vals.at[lats(g * per, per)], vals.at[lats(slot * ns + g * per, per)],
                     f_out.at[2 * side + 1], f_in.at[2 * side + 1, g], f),
        )

    for g in range(GROUPS):
        lax.fori_loop(max(1, g * per), (g + 1) * per, arrived, 0)
        for side in range(2):
            for copy in forwards(g, side):
                copy.start()

    level = jnp.full((8, TOKS), time_ref[0], jnp.int32).astype(F32)
    step_size = (sigma_of(level - 1.0) - sigma_of(level))[0:1, :]
    latent_t = latent_ref[...]

    weighted[LAT:, 0:toks] = jnp.ones((SUMS, toks), BF16)
    for j in range(ns):
        weighted[0:LAT, j * TOKS:(j + 1) * TOKS] = vals[j * LAT:(j + 1) * LAT, :]

    has = (
        jnp.where(jnp.logical_and(back_ref[0] >= 1, place >= 1), 1.0, 0.0),
        jnp.where(jnp.logical_and(ahead_ref[0] >= 1, place <= nf - 2), 1.0, 0.0),
    )
    for side in range(2):
        slot = 1 + side
        for g in range(GROUPS):
            for copy in forwards(g, side):
                copy.wait_recv()
        yes = jnp.full((TOKS, TOKS), has[side], F32)
        no = (1.0 - yes).astype(BF16)
        yes = yes.astype(BF16)
        weighted[LAT:, slot * toks:(slot + 1) * toks] = jnp.full((SUMS, toks), has[side], F32).astype(BF16)
        for j in range(ns):
            k = slot * ns + j
            keys[k * TOKS:(k + 1) * TOKS, :] = (
                keys[k * TOKS:(k + 1) * TOKS, :] * yes + keys[j * TOKS:(j + 1) * TOKS, :] * no)
            weighted[0:LAT, k * TOKS:(k + 1) * TOKS] = vals[k * LAT:(k + 1) * LAT, :] * yes[0:LAT]

    chunks = 3 * toks // CHUNK
    blocks = ns // 2

    def wait_q(b):
        for j in (2 * b, 2 * b + 1):
            if not isinstance(j, int) or j > 0:
                to_seq(qbuf.at[rows(j)], qbuf.at[rows(j)], q_out, q_in.at[j], here).wait_recv()
        return qbuf[pl.ds(pl.multiple_of(b * PAIR, PAIR), PAIR), :]

    def score(q, c, held, top):
        s = lax.dot_general(keys[c * CHUNK:(c + 1) * CHUNK, :], q, (((1,), (1,)), ((), ())),
                            preferred_element_type=F32)
        held[c * CHUNK:(c + 1) * CHUNK, :] = s
        t = jnp.max(s.reshape(CHUNK // 8, 8, PAIR), axis=0)
        return t if top is None else jnp.maximum(top, t)

    def gather(m, c, held, acc):
        p = jnp.exp2(held[c * CHUNK:(c + 1) * CHUNK, :] * RATE - m).astype(BF16)
        r = jnp.dot(weighted[:, c * CHUNK:(c + 1) * CHUNK], p, preferred_element_type=F32)
        return r if acc is None else acc + r

    def straight(j):
        return to_seq(osend.at[lats(j)], obuf.at[lats(j)], o_out.at[j], o_in.at[j], owner(j))

    def finish(b, acc):
        out = acc[0:LAT] / acc[LAT:LAT + 1]
        for i in range(2):
            j = 2 * b + i
            part = out[:, i * TOKS:(i + 1) * TOKS]
            osend[lats(j), :] = part.astype(BF16)
            if i == 0:
                @pl.when(j == 0)
                def _():
                    own[...] = part

            @pl.when(j > 0)
            def _():
                straight(j).start()

    def peak(top):
        return jnp.max(top, axis=0, keepdims=True) * RATE

    def both(b_next, held_next, b, m, held):
        q = wait_q(b_next)
        top = acc = None
        for c in range(chunks):
            top = score(q, c, held_next, top)
            acc = gather(m, c, held, acc)
        finish(b, acc)
        return peak(top)

    q = wait_q(0)
    top = None
    for c in range(chunks):
        top = score(q, c, s0, top)
    m = peak(top)

    def two(i, m):
        m = both(2 * i + 1, s1, 2 * i, m, s0)
        return both(2 * i + 2, s0, 2 * i + 1, m, s1)

    m = lax.fori_loop(0, blocks // 2 - 1, two, m)
    m = both(blocks - 1, s1, blocks - 2, m, s0)
    acc = None
    for c in range(chunks):
        acc = gather(m, c, s1, acc)
    finish(blocks - 1, acc)

    total = own[...]
    for j in range(1, ns):
        to_seq(obuf.at[lats(j)], obuf.at[lats(j)], o_out.at[j], o_in.at[j], here).wait_recv()
        total = total + obuf[j * LAT:(j + 1) * LAT, :].astype(F32)
    mine[...] = latent_t + step_size * total
    pass_on = to_frame(mine, new_hbm.at[0], m_sems.at[0], m_sems.at[1], before)
    pass_on.start()
    vel_ref[...] = total
    out_vel.start()

    rest = pl.ds(TOKS, (ns - 1) * TOKS)
    rest_lat = pl.ds(LAT, (ns - 1) * LAT)
    to_seq(keys.at[rest], keys.at[rest], k_out, k_in.at[0], here).wait_send()
    to_seq(vals.at[rest_lat], vals.at[rest_lat], v_out, v_in.at[0], here).wait_send()
    to_seq(qbuf.at[rest], qbuf.at[rest], q_out, q_in.at[0], here).wait_send()
    for j in range(1, ns):
        to_seq(osend.at[lats(j)], osend.at[lats(j)], o_out.at[j], o_in.at[j], here).wait_send()
    for side in range(2):
        whole = pl.ds(0, toks)
        whole_lat = pl.ds(0, ns * LAT)
        to_frame(keys.at[whole], keys.at[whole], f_out.at[2 * side], f_in.at[0, 0], place).wait_send()
        to_frame(vals.at[whole_lat], vals.at[whole_lat], f_out.at[2 * side + 1], f_in.at[0, 0], place).wait_send()
    pass_on.wait()
    out_vel.wait()


def closing(nf, vel_ref, arrived_ref, noise_ref, vel_out, new_out):
    last = jnp.full((LAT, TOKS), lax.axis_index("frame"), jnp.int32) == nf - 1
    vel_out[...] = vel_ref[...]
    new_out[0] = jnp.where(last, noise_ref[...], arrived_ref[0])


def on_device(nf, ns, queries, key_proj, values, back_count, ahead_count, timestep, latent, noise_frame, w_final):
    anywhere = pl.BlockSpec(memory_space=pltpu.HBM)
    toks = ns * TOKS
    dma = pltpu.SemaphoreType.DMA
    out = jax.ShapeDtypeStruct((1, LAT, TOKS), F32)
    pairs = 2 * toks * 3 * toks
    velocity, arrived = pl.pallas_call(
        functools.partial(kernel, ns, nf),
        out_shape=(out, out),
        in_specs=[anywhere] * 8,
        out_specs=(anywhere, anywhere),
        scratch_shapes=[
            pltpu.SMEM((1,), jnp.int32),
            pltpu.SMEM((1,), jnp.int32),
            pltpu.SMEM((1,), jnp.int32),
            pltpu.VMEM((TOKS, ns * HD), BF16),
            pltpu.VMEM((LAT, ns * HD), BF16),
            pltpu.VMEM((LAT, TOKS), F32),
            pltpu.VMEM((LAT, TOKS), F32),
            pltpu.VMEM((3 * toks, HD), BF16),
            pltpu.VMEM((3 * ns * LAT, TOKS), BF16),
            pltpu.VMEM((ns * LAT, TOKS), BF16),
            pltpu.VMEM((LAT + SUMS, 3 * toks), BF16),
            pltpu.VMEM((toks, HD), BF16),
            pltpu.VMEM((ns * LAT, TOKS), BF16),
            pltpu.VMEM((ns * LAT, TOKS), BF16),
            pltpu.VMEM((LAT, TOKS), F32),
            pltpu.VMEM((LAT, TOKS), F32),
            pltpu.VMEM((3 * toks, PAIR), F32),
            pltpu.VMEM((3 * toks, PAIR), F32),
            dma((9,)), dma, dma, dma, dma((ns,)), dma((4,)), dma((2,)),
            dma((ns,)), dma((ns,)), dma((ns,)), dma((ns,)), dma((4, GROUPS)),
        ],
        compiler_params=pltpu.CompilerParams(
            collective_id=0, has_side_effects=True, vmem_limit_bytes=(64 << 20) - (400 << 10)),
        cost_estimate=pl.CostEstimate(
            flops=pairs * (HD + LAT), bytes_accessed=4 << 20, transcendentals=pairs // 2),
    )(back_count, ahead_count, timestep, queries, key_proj, values,
      w_final.T, jnp.swapaxes(latent, 1, 2))
    velocity, new_queue = pl.pallas_call(
        functools.partial(closing, nf),
        out_shape=(out, out),
        in_specs=[pl.BlockSpec(memory_space=pltpu.VMEM)] * 3,
        out_specs=(pl.BlockSpec(memory_space=pltpu.VMEM),) * 2,
    )(velocity, arrived, noise_frame.T)
    return jnp.swapaxes(velocity, 1, 2), jnp.swapaxes(new_queue, 1, 2)


def solution(mesh):
    nf, ns = mesh.shape["frame"], mesh.shape["seq"]
    spread = P("frame", "seq", None)
    placed = (spread, spread, spread, P("frame"), P("frame"), P("frame"), spread, P("seq", None), P())
    return jax.shard_map(
        functools.partial(on_device, nf, ns),
        mesh=mesh,
        in_specs=placed,
        out_specs=(spread, spread),
        check_vma=False,
    )
```
